32 devices in a mesh: aux: 8 (over z, y), occ: 4 (over x, core).
Axes of the slice: x: 2, y: 2, z: 4, core: 2. Of those that a mesh axis runs over, the one named last changes fastest.
Arguments:
- integrals: bfloat16 [128, 32, 16384], P('aux', 'occ'), may hold values from -6 to 6
- metric_factor: bfloat16 [256, 8], P(('aux', 'occ')), may hold values from -2 to 2
- coefficients: bfloat16 [2048, 128], P(None, 'occ'), may hold values from -0.5 to 0.5
- owners: int32 [128, 1], replicated, may hold values from 0 to 7; in each aligned block of 16 rows (0 to 15, 16 to 31, ...) at most 2 rows name the same one
- row_block: int32 [128], replicated, may hold values from 0 to 1
- column_block: int32 [128], replicated, may hold values from 0 to 15
- screen_counts: int32 [128], replicated, may hold values from 1 to 8
Outputs:
- exchange_blocks: float32 [16, 16384], P('aux')
The draws below stay inside these ranges and needn't reach their ends.
Inputs may be any that keep to these rules, and one draw needn't show every extreme that they name: `owners`: in each aligned block of 16 rows (the pair blocks of one auxiliary device) no owner is named more than 2 times, a bound that some block reaches.
All inputs are finite; a program needn't handle non-finite values.
Results may differ from the reference program's by a relative error of at most 0.0011.
Values may be sent and summed in bfloat16 or wider, within the bound.
A program may use at most 128 MiB of HBM per device.

```python
import math
import jax
import jax.numpy as jnp
import numpy as np
from jax import lax

BF = 128
AQ = 8
SLOTS = 16
CAP = 2
NBLK_DEV = 2
OCC = 128
NB_TOTAL = 16
NBASIS = 2048
N_AUX = 8
N_OCC = 4


def plant(values, own_key, smallest, largest):
    longest = values.shape.index(max(values.shape))
    spots = []
    for shift in (0, 1):
        where = [jax.random.randint(jax.random.fold_in(own_key, axis), (), 0, length) for axis, length in enumerate(values.shape)]
        where[longest] = (where[longest] + shift) % values.shape[longest]
        spots.append(tuple(where))
    return values.at[spots[0]].set(smallest).at[spots[1]].set(largest)


def shard_levels(own_key, dims, pieces, smallest, largest):
    level = 1.0
    for axis_at, parts in pieces:
        heights = jax.random.uniform(jax.random.fold_in(jax.random.fold_in(own_key, 6), axis_at), (parts,), jnp.float32, smallest / len(pieces), largest / len(pieces))
        level = level * jnp.repeat(jnp.exp(heights), dims[axis_at] // parts).reshape((-1,) + (1,) * (len(dims) - 1 - axis_at))
    return level


def assign_block(rng, own, number, rows, count, top, bound, lean):
    order = jax.random.permutation(rng, count)
    packed, ordinary = shares(count, rows * top, bound, lean, True), shares(count, rows * top, bound, lean, False)
    places = jnp.arange(count)

    def named(lengths, offset_by):
        used = int((lengths > 0).sum())
        fixed = max(1, used // 4)
        shifted = fixed + (places - fixed + offset_by * (used - fixed)) % max(1, count - fixed)
        return jnp.zeros((count,), jnp.int32).at[order[jnp.where(places < fixed, places, shifted)]].set(jnp.asarray(lengths, jnp.int32))

    lengths = jnp.where(number % 4 == 0, named(packed, number // 4), named(ordinary, number - number // 4 - 1))
    mixed = jax.random.permutation(jax.random.fold_in(own, 3), count)
    giver, taker = mixed[0:count // 2 * 2:2], mixed[1:count // 2 * 2:2]
    room = jnp.minimum(lengths[giver] - 1, bound - lengths[taker]) // 2
    room = jnp.where((giver == order[0]) | (taker == order[0]) | (lengths[taker] == 0), 0, jnp.maximum(room, 0))
    shifted = jax.random.randint(jax.random.fold_in(own, 4), (count // 2,), 0, 1 << 20) % (room + 1)
    lengths = lengths.at[giver].add(-shifted).at[taker].add(shifted)
    labels = jnp.searchsorted(jnp.cumsum(lengths), jnp.arange(rows * top), side="right").astype(jnp.int32)
    grid = labels.reshape(top, rows).T
    grid = grid[jax.random.permutation(jax.random.fold_in(own, 1), rows)]
    offset_by = jax.random.randint(jax.random.fold_in(own, 2), (rows, 1), 0, top)
    return jnp.take_along_axis(grid, (jnp.arange(top)[None, :] + offset_by) % top, axis=1)


def shares(number_of, total, limit, slope, full):
    loads = [(1 << 20) // math.isqrt(standing ** slope) + 1 for standing in range(1, number_of + 1)]
    largest = limit if full else min(limit, max(-(-total // number_of), total * loads[0] // sum(loads)))
    least = 1 if total - largest >= number_of - 1 else 0
    given, spare = [largest] + [least] * (number_of - 1), total - largest - least * (number_of - 1)
    while spare > 0:
        movable = [i for i in range(1, number_of) if given[i] < largest] or [i for i in range(1, number_of) if given[i] < limit]
        mass, budget = sum([loads[i] for i in movable]), spare
        for i in movable:
            addition = min(limit - given[i], max(1, budget * loads[i] // mass), spare)
            given[i] = given[i] + addition
            spare = spare - addition
    return np.array(given)


def centred(own_key, shape, scale, bound, cuts=(), kind=jnp.bfloat16):
    values = jax.random.normal(own_key, shape, jnp.float32) * scale
    if len(cuts) > 0:
        values = shard_levels(own_key, shape, cuts, -0.22, 0.18) * values
    return jnp.clip(values, min=-bound, max=bound).astype(kind)


def setup_inputs(seed: int = 0) -> dict:
    arg_keys = jax.random.split(jax.random.key(seed), 8)
    integrals = centred(arg_keys[0], (N_AUX * SLOTS, N_OCC * AQ, BF * BF), 1.0, 6.0, ((0, 8), (1, 4)))
    metric_factor = centred(arg_keys[1], (N_AUX * N_OCC * AQ, AQ), AQ ** -0.5, 2.0, ((0, 32),))
    coefficients = centred(arg_keys[2], (NBASIS, OCC), BF ** -0.5, 0.5, ((1, 4),))
    owners_keys = jax.random.split(jax.random.fold_in(arg_keys[3], 1), (N_AUX * SLOTS) // SLOTS)
    owners_turns = jax.random.permutation(jax.random.fold_in(arg_keys[3], 3), (N_AUX * SLOTS) // SLOTS)
    owners = jax.vmap(lambda own, number: assign_block(jax.random.fold_in(arg_keys[3], 2), own, number, SLOTS, N_AUX, 1, CAP, 2))(owners_keys, owners_turns).reshape((N_AUX * SLOTS, 1))
    row_block = plant(jax.random.randint(arg_keys[4], (N_AUX * SLOTS,), 0, NBLK_DEV), jax.random.fold_in(arg_keys[4], 1), 0, NBLK_DEV - 1).astype(jnp.int32)
    column_block = plant(jax.random.randint(arg_keys[5], (N_AUX * SLOTS,), 0, NB_TOTAL), jax.random.fold_in(arg_keys[5], 1), 0, NB_TOTAL - 1).astype(jnp.int32)
    screen_counts = plant(jax.random.randint(arg_keys[6], (N_AUX * SLOTS,), 1, AQ + 1), jax.random.fold_in(arg_keys[6], 1), 1, AQ).astype(jnp.int32)
    return {"integrals": integrals, "metric_factor": metric_factor, "coefficients": coefficients, "owners": owners, "row_block": row_block, "column_block": column_block, "screen_counts": screen_counts}


def reference(integrals, metric_factor, coefficients, owners, row_block, column_block, screen_counts):
    slot_owner = owners[:, 0].astype(jnp.int32)
    block_index = (slot_owner * NBLK_DEV + row_block).astype(jnp.int32)
    earlier = jnp.arange(SLOTS, dtype=jnp.int32)[:, None] > jnp.arange(SLOTS, dtype=jnp.int32)[None, :]
    blocks_view = coefficients.reshape(NB_TOTAL, BF, OCC)
    aux_range = jnp.arange(AQ, dtype=jnp.int32)
    block_range = jnp.arange(NB_TOTAL, dtype=jnp.int32)

    def device_term(total, device):
        source = (device // N_OCC).astype(jnp.int32)
        sub_slab = (device % N_OCC).astype(jnp.int32)
        zero = jnp.zeros((), jnp.int32)
        slab = lax.dynamic_slice(integrals, (source * SLOTS, sub_slab * AQ, zero), (SLOTS, AQ, BF * BF))
        factor = lax.dynamic_slice(metric_factor, (device * AQ, zero), (AQ, AQ))
        local_counts = lax.dynamic_slice(screen_counts, (source * SLOTS,), (SLOTS,))
        local_blocks = lax.dynamic_slice(block_index, (source * SLOTS,), (SLOTS,))
        local_cols = lax.dynamic_slice(column_block, (source * SLOTS,), (SLOTS,))
        live_rows = aux_range[None, :] < local_counts[:, None]
        masked = jnp.where(live_rows[:, :, None], slab, jnp.zeros_like(slab))
        fitted = jnp.einsum("jpc,pq->jqc", masked.astype(jnp.float32), factor.astype(jnp.float32)).astype(jnp.bfloat16)
        column_rows = blocks_view[local_cols].astype(jnp.float32)
        halves = jnp.einsum("jrn,jno->jro", fitted.reshape(SLOTS, AQ * BF, BF).astype(jnp.float32), column_rows).astype(jnp.bfloat16)
        same_block = local_blocks[:, None] == local_blocks[None, :]
        grouped = jnp.dot(same_block.astype(jnp.float32), halves.reshape(SLOTS, -1).astype(jnp.float32), precision=lax.Precision.HIGHEST).astype(jnp.bfloat16)
        grouped = grouped.reshape(SLOTS, AQ, BF, OCC).astype(jnp.float32)
        squares = jnp.einsum("jqmi,jqni->jmn", grouped, grouped)
        leading = jnp.logical_not(jnp.any(same_block & earlier, axis=1))
        selector = ((block_range[:, None] == local_blocks[None, :]) & leading[None, :]).astype(jnp.float32)
        spread = jnp.dot(selector, squares.reshape(SLOTS, BF * BF), precision=lax.Precision.HIGHEST)
        return total + spread, None

    start = jnp.zeros((NB_TOTAL, BF * BF), jnp.float32)
    total, _ = lax.scan(device_term, start, jnp.arange(N_AUX * N_OCC, dtype=jnp.int32))
    return total * (1.0 / (OCC * AQ))
```

```python
import functools

import jax
import jax.numpy as jnp
from jax import lax
from jax.experimental import pallas as pl
from jax.experimental.pallas import tpu as pltpu
from jax.sharding import PartitionSpec as P

BF = 128
NBLK_DEV = 2
CORES = 2
EXTRA = 8
LAG1 = 3
LAG2 = 6
MESH = pl.DeviceIdType.MESH
NT = (((1,), (1,)), ((), ()))


def kernel(
    n_aux, n_occ, owners, rows_in, cols_in, counts,
    x_hbm, factor, coef_hbm, out,
    x, fit, coef, mix, part, r1, held, r2, mine, r3, fin,
    x_sem, c_local, c_send, c_recv, s1, v1, s2, v2, s3, v3, s4, v4,
):
    slots, stacked, _ = x.shape
    aux_local = factor.shape[0]
    occ_local = coef_hbm.shape[0]
    occ_all = n_occ * occ_local
    n_x = n_occ // CORES
    chunk = BF // n_occ
    group = 256 // aux_local
    scale = 1.0 / (occ_all * aux_local)
    me, oc = lax.axis_index("aux"), lax.axis_index("occ")
    mx, mc = lax.div(oc, CORES), lax.rem(oc, CORES)
    spot = mc * n_x + mx

    def x_copy(j):
        return pltpu.make_async_copy(x_hbm.at[j], x.at[j], x_sem.at[j])

    def own_coef(b):
        return pltpu.make_async_copy(
            coef_hbm.at[:, b * BF:(b + 1) * BF], coef.at[oc, b], c_local.at[b])

    for b in range(coef.shape[1]):
        own_coef(b).start()
    for j in range(slots):
        x_copy(j).start()

    barrier = pltpu.get_barrier_semaphore()
    for e in range(1, n_occ):
        pl.semaphore_signal(barrier, inc=1, device_id=(me, lax.rem(oc + e, n_occ)), device_id_type=MESH)
    for k in range(n_aux - 1):
        pl.semaphore_signal(barrier, inc=1, device_id=(lax.rem(me + 1 + k, n_aux), oc), device_id_type=MESH)
    pl.semaphore_wait(barrier, n_occ - 1 + n_aux - 1)

    def c_copy(e):
        return pltpu.make_async_remote_copy(
            src_ref=coef.at[oc], dst_ref=coef.at[oc],
            send_sem=c_send.at[e - 1], recv_sem=c_recv.at[e - 1],
            device_id=(me, lax.rem(oc + e, n_occ)), device_id_type=MESH)

    for b in range(coef.shape[1]):
        own_coef(b).wait()
    for e in range(1, n_occ):
        c_copy(e).start()

    side = group * aux_local
    r = lax.broadcasted_iota(jnp.int32, (side, aux_local), 0)
    q = lax.broadcasted_iota(jnp.int32, (side, aux_local), 1)
    spread = jnp.where(r // group == q, 1.0, 0.0).astype(jnp.bfloat16)
    left = lax.dot_general(spread, factor[...], NT, preferred_element_type=jnp.float32).astype(jnp.bfloat16)
    spread = jnp.where(r % aux_local == q, 1.0, 0.0).astype(jnp.bfloat16)
    both = lax.dot_general(left, spread, NT, preferred_element_type=jnp.float32)
    r = lax.broadcasted_iota(jnp.int32, (side, side), 0)
    q = lax.broadcasted_iota(jnp.int32, (side, side), 1)
    mix[...] = jnp.where(r % group == q // aux_local, both, 0.0).astype(jnp.bfloat16)
    aux_of = lax.broadcasted_iota(jnp.int32, (1, side), 1) % aux_local

    def fit_one(j, _):
        x_copy(j).wait()
        live = jnp.where(aux_of < counts[me * slots + j], 1.0, 0.0).astype(jnp.bfloat16)
        factors = mix[...] * live
        for g in range(stacked // side):
            f = jnp.dot(factors, x[j, g * side:(g + 1) * side, :], preferred_element_type=jnp.float32)
            fit[j, :, g * group:(g + 1) * group, :] = f.astype(jnp.bfloat16).reshape(aux_local, group, BF)
        return 0

    lax.fori_loop(0, slots, fit_one, 0)

    for e in range(1, n_occ):
        c_copy(e).wait_recv()

    rr = lax.broadcasted_iota(jnp.int32, (BF, BF), 0)
    cc = lax.broadcasted_iota(jnp.int32, (BF, BF), 1)

    def compute(k):
        w = lax.rem(me + 1 + k, n_aux)
        j1, j2 = jnp.int32(slots), jnp.int32(-1)
        for j in range(slots):
            hit = owners[me * slots + j] == w
            j1 = jnp.where(hit, jnp.minimum(j1, j), j1)
            j2 = jnp.where(hit, j, j2)
        p1 = j2 >= 0
        p2 = jnp.logical_and(p1, j1 != j2)
        j1, j2 = jnp.where(p1, j1, 0), jnp.where(p1, j2, 0)
        row1, row2 = rows_in[me * slots + j1], rows_in[me * slots + j2]
        b1, b2 = cols_in[me * slots + j1], cols_in[me * slots + j2]
        f = jnp.concatenate([fit[j1].reshape(aux_local * BF, BF), fit[j2].reshape(aux_local * BF, BF)], axis=1)
        c1 = jnp.concatenate([coef[o, b1] for o in range(n_occ)], axis=0)
        c2 = jnp.concatenate([coef[o, b2] for o in range(n_occ)], axis=0)

        def weigh(c, present, row, which):
            on = jnp.where(jnp.logical_and(present, row == which), 1.0, 0.0)
            return c * on.astype(jnp.bfloat16)

        weights = jnp.concatenate([
            jnp.concatenate([weigh(c1, p1, row1, which), weigh(c2, p2, row2, which)], axis=1)
            for which in range(NBLK_DEV)], axis=0)
        grouped = lax.dot_general(f, weights, NT, preferred_element_type=jnp.float32).astype(jnp.bfloat16)
        squares = []
        for which in range(NBLK_DEV):
            g = jnp.concatenate([
                grouped[a * BF:(a + 1) * BF, which * occ_all:(which + 1) * occ_all]
                for a in range(aux_local)], axis=1)
            squares.append(lax.dot_general(g, g, NT, preferred_element_type=jnp.float32) * scale)
        packed = jnp.where(rr >= cc, squares[0], squares[1])
        diag = jnp.sum(jnp.where(rr == cc, squares[1], 0.0), axis=0, keepdims=True)
        tail = jnp.broadcast_to(diag, (EXTRA, BF))
        for c in range(CORES):
            for i in range(n_x):
                at = (c * n_x + i) * chunk
                part[k, c, i, 0:chunk, :] = packed[at:at + chunk]
                part[k, c, i, chunk:chunk + EXTRA, :] = tail

    def copy1(k):
        return pltpu.make_async_remote_copy(
            src_ref=part.at[k, 1 - mc], dst_ref=r1.at[k],
            send_sem=s1.at[k], recv_sem=v1.at[k],
            device_id=(me, mx * CORES + 1 - mc), device_id_type=MESH)

    def copy2(k, d):
        to = lax.rem(mx + d, n_x)
        return pltpu.make_async_remote_copy(
            src_ref=held.at[k, to], dst_ref=r2.at[k, d - 1],
            send_sem=s2.at[k, d - 1], recv_sem=v2.at[k, d - 1],
            device_id=(me, to * CORES + mc), device_id_type=MESH)

    def copy3(k):
        return pltpu.make_async_remote_copy(
            src_ref=mine.at[k], dst_ref=r3.at[k],
            send_sem=s3.at[k], recv_sem=v3.at[k],
            device_id=(lax.rem(me + 1 + k, n_aux), oc), device_id_type=MESH)

    def copy4(e):
        return pltpu.make_async_remote_copy(
            src_ref=fin.at[spot], dst_ref=fin.at[spot],
            send_sem=s4.at[e - 1], recv_sem=v4.at[e - 1],
            device_id=(me, lax.rem(oc + e, n_occ)), device_id_type=MESH)

    def step(t, _):
        @pl.when(t < n_aux)
        def _():
            compute(t)
            copy1(t).start()

        @pl.when(jnp.logical_and(t >= LAG1, t < n_aux + LAG1))
        def _():
            k = t - LAG1
            copy1(k).wait_recv()
            held[k] = part[k, mc] + r1[k]
            for d in range(1, n_x):
                copy2(k, d).start()

        @pl.when(t >= LAG2)
        def _():
            k = t - LAG2
            total = held[k, mx]
            for d in range(1, n_x):
                copy2(k, d).wait_recv()
                total = total + r2[k, d - 1]
            mine[k] = total

            @pl.when(k < n_aux - 1)
            def _():
                copy3(k).start()
        return 0

    lax.fori_loop(0, n_aux + LAG2, step, 0)

    def gather3(k, total):
        copy3(k).wait_recv()
        return total + r3[k]

    fin[spot] = lax.fori_loop(0, n_aux - 1, gather3, mine[n_aux - 1])
    for e in range(1, n_occ):
        copy4(e).start()

    def drain(k, _):
        copy1(k).wait_send()
        for d in range(1, n_x):
            copy2(k, d).wait_send()

        @pl.when(k < n_aux - 1)
        def _():
            copy3(k).wait_send()
        return 0

    lax.fori_loop(0, n_aux, drain, 0)
    for e in range(1, n_occ):
        c_copy(e).wait_send()
    for e in range(1, n_occ):
        copy4(e).wait_recv()
    whole = jnp.concatenate([fin[i, 0:chunk, :] for i in range(n_occ)], axis=0)
    turned = whole.T
    out[0] = jnp.where(rr >= cc, whole, turned)
    out[1] = jnp.where(rr == cc, fin[0, chunk:chunk + 1, :], jnp.where(rr < cc, whole, turned))
    for e in range(1, n_occ):
        copy4(e).wait_send()


def body(integrals, metric_factor, coefficients, owners, row_block, column_block, screen_counts):
    n_aux, n_occ = lax.axis_size("aux"), lax.axis_size("occ")
    slots, aux_local, flat = integrals.shape
    nbasis, occ_local = coefficients.shape
    stacked = integrals.reshape(slots, aux_local, BF, BF).transpose(0, 2, 1, 3).reshape(slots, aux_local * BF, BF)
    n_x = n_occ // CORES
    rows = BF // n_occ + EXTRA
    occ_all = n_occ * occ_local
    dma = pltpu.SemaphoreType.DMA
    f32, bf16 = jnp.float32, jnp.bfloat16
    smem = pl.BlockSpec(memory_space=pltpu.SMEM)
    vmem = pl.BlockSpec(memory_space=pltpu.VMEM)
    hbm = pl.BlockSpec(memory_space=pl.ANY)
    flops = 2 * slots * aux_local * BF * (256 * BF + 2 * BF * occ_all)
    out = pl.pallas_call(
        functools.partial(kernel, n_aux, n_occ),
        out_shape=jax.ShapeDtypeStruct((NBLK_DEV, BF, BF), f32),
        in_specs=[smem] * 4 + [hbm, vmem, hbm],
        out_specs=vmem,
        scratch_shapes=[
            pltpu.VMEM((slots, aux_local * BF, BF), bf16),
            pltpu.VMEM((slots, aux_local, BF, BF), bf16),
            pltpu.VMEM((n_occ, nbasis // BF, occ_local, BF), bf16),
            pltpu.VMEM((256, 256), bf16),
            pltpu.VMEM((n_aux, CORES, n_x, rows, BF), f32),
            pltpu.VMEM((n_aux, n_x, rows, BF), f32),
            pltpu.VMEM((n_aux, n_x, rows, BF), f32),
            pltpu.VMEM((n_aux, n_x - 1, rows, BF), f32),
            pltpu.VMEM((n_aux, rows, BF), f32),
            pltpu.VMEM((n_aux - 1, rows, BF), f32),
            pltpu.VMEM((n_occ, rows, BF), f32),
            dma((slots,)), dma((nbasis // BF,)),
            dma((n_occ - 1,)), dma((n_occ - 1,)),
            dma((n_aux,)), dma((n_aux,)),
            dma((n_aux, n_x - 1)), dma((n_aux, n_x - 1)),
            dma((n_aux - 1,)), dma((n_aux - 1,)),
            dma((n_occ - 1,)), dma((n_occ - 1,)),
        ],
        compiler_params=pltpu.CompilerParams(
            collective_id=0, has_side_effects=True, vmem_limit_bytes=61 * 1024 * 1024),
        cost_estimate=pl.CostEstimate(
            flops=flops, bytes_accessed=integrals.size * 2, transcendentals=0),
    )(owners.reshape(-1), row_block, column_block, screen_counts, stacked, metric_factor, coefficients.T)
    return out.reshape(NBLK_DEV, BF * BF)


def solution(mesh):
    return jax.shard_map(
        body,
        mesh=mesh,
        in_specs=(
            P("aux", "occ", None),
            P(("aux", "occ"), None),
            P(None, "occ"),
            P(),
            P(),
            P(),
            P(),
        ),
        out_specs=P("aux", None),
        check_vma=False,
    )
```

```python
import functools

import jax
import jax.numpy as jnp
from jax import lax
from jax.experimental import pallas as pl
from jax.experimental.pallas import tpu as pltpu
from jax.sharding import PartitionSpec as P

BF = 128
NBLK_DEV = 2
CORES = 2
EXTRA = 8
LAG1 = 3
LAG2 = 6
MESH = pl.DeviceIdType.MESH
NT = (((1,), (1,)), ((), ()))


def kernel(
    n_aux, n_occ, owners_hbm, rows_hbm, cols_hbm, counts_hbm,
    x_hbm, factor_hbm, coef_hbm, out,
    owners, rows_in, cols_in, counts, factor, small_sem,
    x, fit, coef, mix, part, r1, held, r2, mine, r3, fin,
    x_sem, c_local, c_send, c_recv, s1, v1, s2, v2, s3, v3, s4, v4,
):
    slots, stacked, _ = x.shape
    aux_local = factor.shape[0]
    occ_local = coef_hbm.shape[0]
    occ_all = n_occ * occ_local
    n_x = n_occ // CORES
    chunk = BF // n_occ
    group = 256 // aux_local
    scale = 1.0 / (occ_all * aux_local)
    me, oc = lax.axis_index("aux"), lax.axis_index("occ")
    mx, mc = lax.div(oc, CORES), lax.rem(oc, CORES)
    spot = mc * n_x + mx

    def x_copy(j):
        return pltpu.make_async_copy(x_hbm.at[j], x.at[j], x_sem.at[j])

    def own_coef(b):
        return pltpu.make_async_copy(
            coef_hbm.at[:, b * BF:(b + 1) * BF], coef.at[oc, b], c_local.at[b])

    for b in range(coef.shape[1]):
        own_coef(b).start()
    small = [
        pltpu.make_async_copy(a, b, small_sem.at[i])
        for i, (a, b) in enumerate([
            (factor_hbm, factor), (counts_hbm, counts), (owners_hbm, owners),
            (rows_hbm, rows_in), (cols_hbm, cols_in)])]
    for copy in small:
        copy.start()
    for j in range(slots):
        x_copy(j).start()

    barrier = pltpu.get_barrier_semaphore()
    for e in range(1, n_occ):
        pl.semaphore_signal(barrier, inc=1, device_id=(me, lax.rem(oc + e, n_occ)), device_id_type=MESH)
    for k in range(n_aux - 1):
        pl.semaphore_signal(barrier, inc=1, device_id=(lax.rem(me + 1 + k, n_aux), oc), device_id_type=MESH)
    pl.semaphore_wait(barrier, n_occ - 1 + n_aux - 1)

    def c_copy(e):
        if e == 0:
            what, to = oc, mx * CORES + 1 - mc
        elif e < n_x:
            what, to = oc, lax.rem(mx + e, n_x) * CORES + mc
        else:
            what, to = lax.rem(mx + e + 1, n_x) * CORES + mc, mx * CORES + 1 - mc
        return pltpu.make_async_remote_copy(
            src_ref=coef.at[what], dst_ref=coef.at[what],
            send_sem=c_send.at[e], recv_sem=c_recv.at[e],
            device_id=(me, to), device_id_type=MESH)

    for b in range(coef.shape[1]):
        own_coef(b).wait()
    for e in list(range(1, n_x)) + [0]:
        c_copy(e).start()

    for copy in small:
        copy.wait()

    side = group * aux_local
    r = lax.broadcasted_iota(jnp.int32, (side, aux_local), 0)
    q = lax.broadcasted_iota(jnp.int32, (side, aux_local), 1)
    spread = jnp.where(r // group == q, 1.0, 0.0).astype(jnp.bfloat16)
    left = lax.dot_general(spread, factor[...], NT, preferred_element_type=jnp.float32).astype(jnp.bfloat16)
    spread = jnp.where(r % aux_local == q, 1.0, 0.0).astype(jnp.bfloat16)
    both = lax.dot_general(left, spread, NT, preferred_element_type=jnp.float32)
    r = lax.broadcasted_iota(jnp.int32, (side, side), 0)
    q = lax.broadcasted_iota(jnp.int32, (side, side), 1)
    mix[...] = jnp.where(r % group == q // aux_local, both, 0.0).astype(jnp.bfloat16)
    aux_of = lax.broadcasted_iota(jnp.int32, (1, side), 1) % aux_local

    def fit_one(j, _):
        x_copy(j).wait()
        live = jnp.where(aux_of < counts[me * slots + j], 1.0, 0.0).astype(jnp.bfloat16)
        factors = mix[...] * live
        for g in range(stacked // side):
            f = jnp.dot(factors, x[j, g * side:(g + 1) * side, :], preferred_element_type=jnp.float32)
            fit[j, :, g * group:(g + 1) * group, :] = f.astype(jnp.bfloat16).reshape(aux_local, group, BF)
        return 0

    before = slots * 3 // 4
    lax.fori_loop(0, before, fit_one, 0)
    for e in range(1, n_x):
        c_copy(e).wait_recv()
    for e in range(n_x, n_occ - 1):
        c_copy(e).start()
    lax.fori_loop(before, slots, fit_one, 0)
    c_copy(0).wait_recv()
    for e in range(n_x, n_occ - 1):
        c_copy(e).wait_recv()

    rr = lax.broadcasted_iota(jnp.int32, (BF, BF), 0)
    cc = lax.broadcasted_iota(jnp.int32, (BF, BF), 1)

    def compute(k):
        w = lax.rem(me + 1 + k, n_aux)
        j1, j2 = jnp.int32(slots), jnp.int32(-1)
        for j in range(slots):
            hit = owners[me * slots + j] == w
            j1 = jnp.where(hit, jnp.minimum(j1, j), j1)
            j2 = jnp.where(hit, j, j2)
        p1 = j2 >= 0
        p2 = jnp.logical_and(p1, j1 != j2)
        j1, j2 = jnp.where(p1, j1, 0), jnp.where(p1, j2, 0)
        row1, row2 = rows_in[me * slots + j1], rows_in[me * slots + j2]
        b1, b2 = cols_in[me * slots + j1], cols_in[me * slots + j2]
        f = jnp.concatenate([fit[j1].reshape(aux_local * BF, BF), fit[j2].reshape(aux_local * BF, BF)], axis=1)
        c1 = jnp.concatenate([coef[o, b1] for o in range(n_occ)], axis=0)
        c2 = jnp.concatenate([coef[o, b2] for o in range(n_occ)], axis=0)

        def weigh(c, present, row, which):
            on = jnp.where(jnp.logical_and(present, row == which), 1.0, 0.0)
            return c * on.astype(jnp.bfloat16)

        weights = jnp.concatenate([
            jnp.concatenate([weigh(c1, p1, row1, which), weigh(c2, p2, row2, which)], axis=1)
            for which in range(NBLK_DEV)], axis=0)
        grouped = lax.dot_general(f, weights, NT, preferred_element_type=jnp.float32).astype(jnp.bfloat16)
        squares = []
        for which in range(NBLK_DEV):
            g = jnp.concatenate([
                grouped[a * BF:(a + 1) * BF, which * occ_all:(which + 1) * occ_all]
                for a in range(aux_local)], axis=1)
            squares.append(lax.dot_general(g, g, NT, preferred_element_type=jnp.float32) * scale)
        packed = jnp.where(rr >= cc, squares[0], squares[1])
        diag = jnp.sum(jnp.where(rr == cc, squares[1], 0.0), axis=0, keepdims=True)
        tail = jnp.broadcast_to(diag, (EXTRA, BF))
        for c in range(CORES):
            for i in range(n_x):
                at = (c * n_x + i) * chunk
                part[k, c, i, 0:chunk, :] = packed[at:at + chunk]
                part[k, c, i, chunk:chunk + EXTRA, :] = tail

    def copy1(k):
        return pltpu.make_async_remote_copy(
            src_ref=part.at[k, 1 - mc], dst_ref=r1.at[k],
            send_sem=s1.at[k], recv_sem=v1.at[k],
            device_id=(me, mx * CORES + 1 - mc), device_id_type=MESH)

    def copy2(k, d):
        to = lax.rem(mx + d, n_x)
        return pltpu.make_async_remote_copy(
            src_ref=held.at[k, to], dst_ref=r2.at[k, d - 1],
            send_sem=s2.at[k, d - 1], recv_sem=v2.at[k, d - 1],
            device_id=(me, to * CORES + mc), device_id_type=MESH)

    def copy3(k):
        return pltpu.make_async_remote_copy(
            src_ref=mine.at[k], dst_ref=r3.at[k],
            send_sem=s3.at[k], recv_sem=v3.at[k],
            device_id=(lax.rem(me + 1 + k, n_aux), oc), device_id_type=MESH)

    def copy4(e):
        return pltpu.make_async_remote_copy(
            src_ref=fin.at[spot], dst_ref=fin.at[spot],
            send_sem=s4.at[e - 1], recv_sem=v4.at[e - 1],
            device_id=(me, lax.rem(oc + e, n_occ)), device_id_type=MESH)

    def step(t, _):
        @pl.when(t < n_aux)
        def _():
            compute(t)
            copy1(t).start()

        @pl.when(jnp.logical_and(t >= LAG1, t < n_aux + LAG1))
        def _():
            k = t - LAG1
            copy1(k).wait_recv()
            held[k] = part[k, mc] + r1[k]
            for d in range(1, n_x):
                copy2(k, d).start()

        @pl.when(t >= LAG2)
        def _():
            k = t - LAG2
            total = held[k, mx]
            for d in range(1, n_x):
                copy2(k, d).wait_recv()
                total = total + r2[k, d - 1]
            mine[k] = total

            @pl.when(k < n_aux - 1)
            def _():
                copy3(k).start()
        return 0

    lax.fori_loop(0, n_aux + LAG2, step, 0)

    def gather3(k, total):
        copy3(k).wait_recv()
        return total + r3[k]

    fin[spot] = lax.fori_loop(0, n_aux - 1, gather3, mine[n_aux - 1])
    for e in range(1, n_occ):
        copy4(e).start()

    def drain(k, _):
        copy1(k).wait_send()
        for d in range(1, n_x):
            copy2(k, d).wait_send()

        @pl.when(k < n_aux - 1)
        def _():
            copy3(k).wait_send()
        return 0

    lax.fori_loop(0, n_aux, drain, 0)
    for e in range(n_occ - 1):
        c_copy(e).wait_send()
    for e in range(1, n_occ):
        copy4(e).wait_recv()
    whole = jnp.concatenate([fin[i, 0:chunk, :] for i in range(n_occ)], axis=0)
    turned = whole.T
    out[0] = jnp.where(rr >= cc, whole, turned)
    out[1] = jnp.where(rr == cc, fin[0, chunk:chunk + 1, :], jnp.where(rr < cc, whole, turned))
    for e in range(1, n_occ):
        copy4(e).wait_send()


def body(integrals, metric_factor, coefficients, owners, row_block, column_block, screen_counts):
    n_aux, n_occ = lax.axis_size("aux"), lax.axis_size("occ")
    slots, aux_local, flat = integrals.shape
    nbasis, occ_local = coefficients.shape
    stacked = integrals.reshape(slots, aux_local, BF, BF).transpose(0, 2, 1, 3).reshape(slots, aux_local * BF, BF)
    n_x = n_occ // CORES
    rows = BF // n_occ + EXTRA
    occ_all = n_occ * occ_local
    dma = pltpu.SemaphoreType.DMA
    f32, bf16 = jnp.float32, jnp.bfloat16
    vmem = pl.BlockSpec(memory_space=pltpu.VMEM)
    hbm = pl.BlockSpec(memory_space=pl.ANY)
    flops = 2 * slots * aux_local * BF * (256 * BF + 2 * BF * occ_all)
    out = pl.pallas_call(
        functools.partial(kernel, n_aux, n_occ),
        out_shape=jax.ShapeDtypeStruct((NBLK_DEV, BF, BF), f32),
        in_specs=[hbm] * 7,
        out_specs=vmem,
        scratch_shapes=[
            pltpu.SMEM(row_block.shape, jnp.int32),
            pltpu.SMEM(row_block.shape, jnp.int32),
            pltpu.SMEM(row_block.shape, jnp.int32),
            pltpu.SMEM(row_block.shape, jnp.int32),
            pltpu.VMEM(metric_factor.shape, bf16),
            dma((5,)),
            pltpu.VMEM((slots, aux_local * BF, BF), bf16),
            pltpu.VMEM((slots, aux_local, BF, BF), bf16),
            pltpu.VMEM((n_occ, nbasis // BF, occ_local, BF), bf16),
            pltpu.VMEM((256, 256), bf16),
            pltpu.VMEM((n_aux, CORES, n_x, rows, BF), f32),
            pltpu.VMEM((n_aux, n_x, rows, BF), f32),
            pltpu.VMEM((n_aux, n_x, rows, BF), f32),
            pltpu.VMEM((n_aux, n_x - 1, rows, BF), f32),
            pltpu.VMEM((n_aux, rows, BF), f32),
            pltpu.VMEM((n_aux - 1, rows, BF), f32),
            pltpu.VMEM((n_occ, rows, BF), f32),
            dma((slots,)), dma((nbasis // BF,)),
            dma((n_occ - 1,)), dma((n_occ - 1,)),
            dma((n_aux,)), dma((n_aux,)),
            dma((n_aux, n_x - 1)), dma((n_aux, n_x - 1)),
            dma((n_aux - 1,)), dma((n_aux - 1,)),
            dma((n_occ - 1,)), dma((n_occ - 1,)),
        ],
        compiler_params=pltpu.CompilerParams(
            collective_id=0, has_side_effects=True, vmem_limit_bytes=61 * 1024 * 1024),
        cost_estimate=pl.CostEstimate(
            flops=flops, bytes_accessed=integrals.size * 2, transcendentals=0),
    )(owners.reshape(-1), row_block, column_block, screen_counts, stacked, metric_factor, coefficients.T)
    return out.reshape(NBLK_DEV, BF * BF)


def solution(mesh):
    return jax.shard_map(
        body,
        mesh=mesh,
        in_specs=(
            P("aux", "occ", None),
            P(("aux", "occ"), None),
            P(None, "occ"),
            P(),
            P(),
            P(),
            P(),
        ),
        out_specs=P("aux", None),
        check_vma=False,
    )
```

```python
import functools

import jax
import jax.numpy as jnp
from jax import lax
from jax.experimental import pallas as pl
from jax.experimental.pallas import tpu as pltpu
from jax.sharding import PartitionSpec as P

BF = 128
NBLK_DEV = 2
CORES = 2
EXTRA = 8
LAG1 = 1
LAG2 = 3
MESH = pl.DeviceIdType.MESH
NT = (((1,), (1,)), ((), ()))


def kernel(
    n_aux, n_occ, owners_hbm, rows_hbm, cols_hbm, counts_hbm,
    x_hbm, factor_hbm, coef_hbm, out,
    owners, rows_in, cols_in, counts, factor, small_sem,
    x, fit, coef, mix, part, r1, held, r2, mine, r3, fin,
    x_sem, c_local, c_send, c_recv, s1, v1, s2, v2, s3, v3, s4, v4,
):
    slots, stacked, _ = x.shape
    aux_local = factor.shape[0]
    occ_local = coef_hbm.shape[0]
    occ_all = n_occ * occ_local
    n_x = n_occ // CORES
    chunk = BF // n_occ
    group = 256 // aux_local
    scale = 1.0 / (occ_all * aux_local)
    me, oc = lax.axis_index("aux"), lax.axis_index("occ")
    mx, mc = lax.div(oc, CORES), lax.rem(oc, CORES)
    spot = mc * n_x + mx

    def x_copy(j):
        return pltpu.make_async_copy(x_hbm.at[j], x.at[j], x_sem.at[j])

    def own_coef(b):
        return pltpu.make_async_copy(
            coef_hbm.at[:, b * BF:(b + 1) * BF], coef.at[oc, b], c_local.at[b])

    for b in range(coef.shape[1]):
        own_coef(b).start()
    small = [
        pltpu.make_async_copy(a, b, small_sem.at[i])
        for i, (a, b) in enumerate([
            (factor_hbm, factor), (counts_hbm, counts), (owners_hbm, owners),
            (rows_hbm, rows_in), (cols_hbm, cols_in)])]
    for copy in small:
        copy.start()
    for j in range(slots):
        x_copy(j).start()

    barrier = pltpu.get_barrier_semaphore()
    for e in range(1, n_occ):
        pl.semaphore_signal(barrier, inc=1, device_id=(me, lax.rem(oc + e, n_occ)), device_id_type=MESH)
    for k in range(n_aux - 1):
        pl.semaphore_signal(barrier, inc=1, device_id=(lax.rem(me + 1 + k, n_aux), oc), device_id_type=MESH)

    def c_copy(e):
        if e == 0:
            what, to = oc, mx * CORES + 1 - mc
        elif e < n_x:
            what, to = oc, lax.rem(mx + e, n_x) * CORES + mc
        else:
            what, to = lax.rem(mx + e + 1, n_x) * CORES + mc, mx * CORES + 1 - mc
        return pltpu.make_async_remote_copy(
            src_ref=coef.at[what], dst_ref=coef.at[what],
            send_sem=c_send.at[e], recv_sem=c_recv.at[e],
            device_id=(me, to), device_id_type=MESH)


    for copy in small:
        copy.wait()

    side = group * aux_local
    r = lax.broadcasted_iota(jnp.int32, (side, aux_local), 0)
    q = lax.broadcasted_iota(jnp.int32, (side, aux_local), 1)
    spread = jnp.where(r // group == q, 1.0, 0.0).astype(jnp.bfloat16)
    left = lax.dot_general(spread, factor[...], NT, preferred_element_type=jnp.float32).astype(jnp.bfloat16)
    spread = jnp.where(r % aux_local == q, 1.0, 0.0).astype(jnp.bfloat16)
    both = lax.dot_general(left, spread, NT, preferred_element_type=jnp.float32)
    r = lax.broadcasted_iota(jnp.int32, (side, side), 0)
    q = lax.broadcasted_iota(jnp.int32, (side, side), 1)
    mix[...] = jnp.where(r % group == q // aux_local, both, 0.0).astype(jnp.bfloat16)
    aux_of = lax.broadcasted_iota(jnp.int32, (1, side), 1) % aux_local

    def fit_one(j, _):
        x_copy(j).wait()
        live = jnp.where(aux_of < counts[me * slots + j], 1.0, 0.0).astype(jnp.bfloat16)
        factors = mix[...] * live
        for g in range(stacked // side):
            f = jnp.dot(factors, x[j, g * side:(g + 1) * side, :], preferred_element_type=jnp.float32)
            fit[j, :, g * group:(g + 1) * group, :] = f.astype(jnp.bfloat16).reshape(aux_local, group, BF)
        return 0

    early = slots * 4 // 16
    lax.fori_loop(0, early, fit_one, 0)
    pl.semaphore_wait(barrier, n_occ - 1 + n_aux - 1)
    for b in range(coef.shape[1]):
        own_coef(b).wait()
    for e in list(range(1, n_x)) + [0]:
        c_copy(e).start()
    before = slots * 12 // 16
    lax.fori_loop(early, before, fit_one, 0)
    for e in range(1, n_x):
        c_copy(e).wait_recv()
    for e in range(n_x, n_occ - 1):
        c_copy(e).start()
    lax.fori_loop(before, slots, fit_one, 0)
    c_copy(0).wait_recv()
    for e in range(n_x, n_occ - 1):
        c_copy(e).wait_recv()

    rr = lax.broadcasted_iota(jnp.int32, (BF, BF), 0)
    cc = lax.broadcasted_iota(jnp.int32, (BF, BF), 1)

    def compute(k):
        w = lax.rem(me + 1 + k, n_aux)
        j1, j2 = jnp.int32(slots), jnp.int32(-1)
        for j in range(slots):
            hit = owners[me * slots + j] == w
            j1 = jnp.where(hit, jnp.minimum(j1, j), j1)
            j2 = jnp.where(hit, j, j2)
        p1 = j2 >= 0
        p2 = jnp.logical_and(p1, j1 != j2)
        j1, j2 = jnp.where(p1, j1, 0), jnp.where(p1, j2, 0)
        row1, row2 = rows_in[me * slots + j1], rows_in[me * slots + j2]
        b1, b2 = cols_in[me * slots + j1], cols_in[me * slots + j2]
        f = jnp.concatenate([fit[j1].reshape(aux_local * BF, BF), fit[j2].reshape(aux_local * BF, BF)], axis=1)
        c1 = jnp.concatenate([coef[o, b1] for o in range(n_occ)], axis=0)
        c2 = jnp.concatenate([coef[o, b2] for o in range(n_occ)], axis=0)

        def weigh(c, present, row, which):
            on = jnp.where(jnp.logical_and(present, row == which), 1.0, 0.0)
            return c * on.astype(jnp.bfloat16)

        weights = jnp.concatenate([
            jnp.concatenate([weigh(c1, p1, row1, which), weigh(c2, p2, row2, which)], axis=1)
            for which in range(NBLK_DEV)], axis=0)
        grouped = lax.dot_general(f, weights, NT, preferred_element_type=jnp.float32).astype(jnp.bfloat16)
        squares = []
        for which in range(NBLK_DEV):
            g = jnp.concatenate([
                grouped[a * BF:(a + 1) * BF, which * occ_all:(which + 1) * occ_all]
                for a in range(aux_local)], axis=1)
            squares.append(lax.dot_general(g, g, NT, preferred_element_type=jnp.float32) * scale)
        packed = jnp.where(rr >= cc, squares[0], squares[1])
        diag = jnp.sum(jnp.where(rr == cc, squares[1], 0.0), axis=0, keepdims=True)
        tail = jnp.broadcast_to(diag, (EXTRA, BF))
        for c in range(CORES):
            for i in range(n_x):
                at = (c * n_x + i) * chunk
                part[k, c, i, 0:chunk, :] = packed[at:at + chunk]
                part[k, c, i, chunk:chunk + EXTRA, :] = tail

    def copy1(k):
        return pltpu.make_async_remote_copy(
            src_ref=part.at[k, 1 - mc], dst_ref=r1.at[k],
            send_sem=s1.at[k], recv_sem=v1.at[k],
            device_id=(me, mx * CORES + 1 - mc), device_id_type=MESH)

    def copy2(k, d):
        to = lax.rem(mx + d, n_x)
        return pltpu.make_async_remote_copy(
            src_ref=held.at[k, to], dst_ref=r2.at[k, d - 1],
            send_sem=s2.at[k, d - 1], recv_sem=v2.at[k, d - 1],
            device_id=(me, to * CORES + mc), device_id_type=MESH)

    def copy3(k):
        return pltpu.make_async_remote_copy(
            src_ref=mine.at[k], dst_ref=r3.at[k],
            send_sem=s3.at[k], recv_sem=v3.at[k],
            device_id=(lax.rem(me + 1 + k, n_aux), oc), device_id_type=MESH)

    def copy4(e):
        return pltpu.make_async_remote_copy(
            src_ref=fin.at[spot], dst_ref=fin.at[spot],
            send_sem=s4.at[e - 1], recv_sem=v4.at[e - 1],
            device_id=(me, lax.rem(oc + e, n_occ)), device_id_type=MESH)

    pairs = n_aux // 2

    def step(t, _):
        @pl.when(t < pairs)
        def _():
            compute(2 * t)
            compute(2 * t + 1)
            copy1(2 * t).start()
            copy1(2 * t + 1).start()

        @pl.when(jnp.logical_and(t >= LAG1, t < pairs + LAG1))
        def _():
            for i in range(2):
                k = 2 * (t - LAG1) + i
                copy1(k).wait_recv()
                held[k] = part[k, mc] + r1[k]
                for d in range(1, n_x):
                    copy2(k, d).start()

        @pl.when(t >= LAG2)
        def _():
            for i in range(2):
                k = 2 * (t - LAG2) + i
                total = held[k, mx]
                for d in range(1, n_x):
                    copy2(k, d).wait_recv()
                    total = total + r2[k, d - 1]
                mine[k] = total

                @pl.when(k < n_aux - 1)
                def _():
                    copy3(k).start()
        return 0

    lax.fori_loop(0, pairs + LAG2, step, 0)

    def gather3(k, total):
        copy3(k).wait_recv()
        return total + r3[k]

    fin[spot] = lax.fori_loop(0, n_aux - 1, gather3, mine[n_aux - 1])
    for e in range(1, n_occ):
        copy4(e).start()

    def drain(k, _):
        copy1(k).wait_send()
        for d in range(1, n_x):
            copy2(k, d).wait_send()

        @pl.when(k < n_aux - 1)
        def _():
            copy3(k).wait_send()
        return 0

    lax.fori_loop(0, n_aux, drain, 0)
    for e in range(n_occ - 1):
        c_copy(e).wait_send()
    for e in range(1, n_occ):
        copy4(e).wait_recv()
    whole = jnp.concatenate([fin[i, 0:chunk, :] for i in range(n_occ)], axis=0)
    turned = whole.T
    out[0] = jnp.where(rr >= cc, whole, turned)
    out[1] = jnp.where(rr == cc, fin[0, chunk:chunk + 1, :], jnp.where(rr < cc, whole, turned))
    for e in range(1, n_occ):
        copy4(e).wait_send()


def body(integrals, metric_factor, coefficients, owners, row_block, column_block, screen_counts):
    n_aux, n_occ = lax.axis_size("aux"), lax.axis_size("occ")
    slots, aux_local, flat = integrals.shape
    nbasis, occ_local = coefficients.shape
    stacked = integrals.reshape(slots, aux_local, BF, BF).transpose(0, 2, 1, 3).reshape(slots, aux_local * BF, BF)
    n_x = n_occ // CORES
    rows = BF // n_occ + EXTRA
    occ_all = n_occ * occ_local
    dma = pltpu.SemaphoreType.DMA
    f32, bf16 = jnp.float32, jnp.bfloat16
    vmem = pl.BlockSpec(memory_space=pltpu.VMEM)
    hbm = pl.BlockSpec(memory_space=pl.ANY)
    flops = 2 * slots * aux_local * BF * (256 * BF + 2 * BF * occ_all)
    out = pl.pallas_call(
        functools.partial(kernel, n_aux, n_occ),
        out_shape=jax.ShapeDtypeStruct((NBLK_DEV, BF, BF), f32),
        in_specs=[hbm] * 7,
        out_specs=vmem,
        scratch_shapes=[
            pltpu.SMEM(row_block.shape, jnp.int32),
            pltpu.SMEM(row_block.shape, jnp.int32),
            pltpu.SMEM(row_block.shape, jnp.int32),
            pltpu.SMEM(row_block.shape, jnp.int32),
            pltpu.VMEM(metric_factor.shape, bf16),
            dma((5,)),
            pltpu.VMEM((slots, aux_local * BF, BF), bf16),
            pltpu.VMEM((slots, aux_local, BF, BF), bf16),
            pltpu.VMEM((n_occ, nbasis // BF, occ_local, BF), bf16),
            pltpu.VMEM((256, 256), bf16),
            pltpu.VMEM((n_aux, CORES, n_x, rows, BF), f32),
            pltpu.VMEM((n_aux, n_x, rows, BF), f32),
            pltpu.VMEM((n_aux, n_x, rows, BF), f32),
            pltpu.VMEM((n_aux, n_x - 1, rows, BF), f32),
            pltpu.VMEM((n_aux, rows, BF), f32),
            pltpu.VMEM((n_aux - 1, rows, BF), f32),
            pltpu.VMEM((n_occ, rows, BF), f32),
            dma((slots,)), dma((nbasis // BF,)),
            dma((n_occ - 1,)), dma((n_occ - 1,)),
            dma((n_aux,)), dma((n_aux,)),
            dma((n_aux, n_x - 1)), dma((n_aux, n_x - 1)),
            dma((n_aux - 1,)), dma((n_aux - 1,)),
            dma((n_occ - 1,)), dma((n_occ - 1,)),
        ],
        compiler_params=pltpu.CompilerParams(
            collective_id=0, has_side_effects=True, vmem_limit_bytes=61 * 1024 * 1024),
        cost_estimate=pl.CostEstimate(
            flops=flops, bytes_accessed=integrals.size * 2, transcendentals=0),
    )(owners.reshape(-1), row_block, column_block, screen_counts, stacked, metric_factor, coefficients.T)
    return out.reshape(NBLK_DEV, BF * BF)


def solution(mesh):
    return jax.shard_map(
        body,
        mesh=mesh,
        in_specs=(
            P("aux", "occ", None),
            P(("aux", "occ"), None),
            P(None, "occ"),
            P(),
            P(),
            P(),
            P(),
        ),
        out_specs=P("aux", None),
        check_vma=False,
    )
```

```python
import functools

import jax
import jax.numpy as jnp
from jax import lax
from jax.experimental import pallas as pl
from jax.experimental.pallas import tpu as pltpu
from jax.sharding import PartitionSpec as P

BF = 128
NBLK_DEV = 2
CORES = 2
EXTRA = 8
LAG1 = 1
LAG2 = 3
MESH = pl.DeviceIdType.MESH
NT = (((1,), (1,)), ((), ()))


def kernel(
    n_aux, n_occ, owners_hbm, rows_hbm, cols_hbm, counts_hbm,
    x_hbm, factor_hbm, coef_hbm, out,
    owners, rows_in, cols_in, counts, factor, small_sem,
    x, fit, coef, mix, part, r1, held, r2, mine, r3, fin,
    x_sem, c_local, c_send, c_recv, s1, v1, s2, v2, s3, v3, s4, v4,
):
    slots, stacked, _ = x.shape
    aux_local = factor.shape[0]
    occ_local = coef_hbm.shape[0]
    occ_all = n_occ * occ_local
    n_x = n_occ // CORES
    chunk = BF // n_occ
    group = 256 // aux_local
    scale = 1.0 / (occ_all * aux_local)
    me, oc = lax.axis_index("aux"), lax.axis_index("occ")
    mx, mc = lax.div(oc, CORES), lax.rem(oc, CORES)
    spot = mc * n_x + mx

    def x_copy(j):
        return pltpu.make_async_copy(x_hbm.at[j], x.at[j], x_sem.at[j])

    def own_coef(b):
        return pltpu.make_async_copy(
            coef_hbm.at[:, b * BF:(b + 1) * BF], coef.at[oc, b], c_local.at[b])

    for b in range(coef.shape[1]):
        own_coef(b).start()
    small = [
        pltpu.make_async_copy(a, b, small_sem.at[i])
        for i, (a, b) in enumerate([
            (factor_hbm, factor), (counts_hbm, counts), (owners_hbm, owners),
            (rows_hbm, rows_in), (cols_hbm, cols_in)])]
    for copy in small:
        copy.start()
    for j in range(slots):
        x_copy(j).start()

    barrier = pltpu.get_barrier_semaphore()
    for e in range(1, n_occ):
        pl.semaphore_signal(barrier, inc=1, device_id=(me, lax.rem(oc + e, n_occ)), device_id_type=MESH)
    for k in range(n_aux - 1):
        pl.semaphore_signal(barrier, inc=1, device_id=(lax.rem(me + 1 + k, n_aux), oc), device_id_type=MESH)

    def c_copy(e):
        if e == 0:
            what, to = oc, mx * CORES + 1 - mc
        elif e < n_x:
            what, to = oc, lax.rem(mx + e, n_x) * CORES + mc
        else:
            what, to = lax.rem(mx + e + 1, n_x) * CORES + mc, mx * CORES + 1 - mc
        return pltpu.make_async_remote_copy(
            src_ref=coef.at[what], dst_ref=coef.at[what],
            send_sem=c_send.at[e], recv_sem=c_recv.at[e],
            device_id=(me, to), device_id_type=MESH)


    for copy in small:
        copy.wait()

    side = group * aux_local
    r = lax.broadcasted_iota(jnp.int32, (side, aux_local), 0)
    q = lax.broadcasted_iota(jnp.int32, (side, aux_local), 1)
    spread = jnp.where(r // group == q, 1.0, 0.0).astype(jnp.bfloat16)
    left = lax.dot_general(spread, factor[...], NT, preferred_element_type=jnp.float32).astype(jnp.bfloat16)
    spread = jnp.where(r % aux_local == q, 1.0, 0.0).astype(jnp.bfloat16)
    both = lax.dot_general(left, spread, NT, preferred_element_type=jnp.float32)
    r = lax.broadcasted_iota(jnp.int32, (side, side), 0)
    q = lax.broadcasted_iota(jnp.int32, (side, side), 1)
    mix[...] = jnp.where(r % group == q // aux_local, both, 0.0).astype(jnp.bfloat16)
    aux_of = lax.broadcasted_iota(jnp.int32, (1, side), 1) % aux_local

    def fit_one(j, _):
        x_copy(j).wait()
        live = jnp.where(aux_of < counts[me * slots + j], 1.0, 0.0).astype(jnp.bfloat16)
        factors = mix[...] * live
        for g in range(stacked // side):
            f = jnp.dot(factors, x[j, g * side:(g + 1) * side, :], preferred_element_type=jnp.float32)
            fit[j, :, g * group:(g + 1) * group, :] = f.astype(jnp.bfloat16).reshape(aux_local, group, BF)
        return 0

    early = slots * 2 // 16
    lax.fori_loop(0, early, fit_one, 0)
    pl.semaphore_wait(barrier, n_occ - 1 + n_aux - 1)
    for b in range(coef.shape[1]):
        own_coef(b).wait()
    for e in list(range(1, n_x)) + [0]:
        c_copy(e).start()
    before = slots * 12 // 16
    lax.fori_loop(early, before, fit_one, 0)
    for e in range(1, n_x):
        c_copy(e).wait_recv()
    for e in range(n_x, n_occ - 1):
        c_copy(e).start()
    lax.fori_loop(before, slots, fit_one, 0)
    c_copy(0).wait_recv()
    for e in range(n_x, n_occ - 1):
        c_copy(e).wait_recv()

    rr = lax.broadcasted_iota(jnp.int32, (BF, BF), 0)
    cc = lax.broadcasted_iota(jnp.int32, (BF, BF), 1)

    def compute(k):
        w = lax.rem(me + 1 + k, n_aux)
        j1, j2 = jnp.int32(slots), jnp.int32(-1)
        for j in range(slots):
            hit = owners[me * slots + j] == w
            j1 = jnp.where(hit, jnp.minimum(j1, j), j1)
            j2 = jnp.where(hit, j, j2)
        p1 = j2 >= 0
        p2 = jnp.logical_and(p1, j1 != j2)
        j1, j2 = jnp.where(p1, j1, 0), jnp.where(p1, j2, 0)
        row1, row2 = rows_in[me * slots + j1], rows_in[me * slots + j2]
        b1, b2 = cols_in[me * slots + j1], cols_in[me * slots + j2]
        f = jnp.concatenate([fit[j1].reshape(aux_local * BF, BF), fit[j2].reshape(aux_local * BF, BF)], axis=1)
        c1 = jnp.concatenate([coef[o, b1] for o in range(n_occ)], axis=0)
        c2 = jnp.concatenate([coef[o, b2] for o in range(n_occ)], axis=0)

        def weigh(c, present, row, which):
            on = jnp.where(jnp.logical_and(present, row == which), 1.0, 0.0)
            return c * on.astype(jnp.bfloat16)

        weights = jnp.concatenate([
            jnp.concatenate([weigh(c1, p1, row1, which), weigh(c2, p2, row2, which)], axis=1)
            for which in range(NBLK_DEV)], axis=0)
        grouped = lax.dot_general(f, weights, NT, preferred_element_type=jnp.float32).astype(jnp.bfloat16)
        squares = []
        for which in range(NBLK_DEV):
            g = jnp.concatenate([
                grouped[a * BF:(a + 1) * BF, which * occ_all:(which + 1) * occ_all]
                for a in range(aux_local)], axis=1)
            squares.append(lax.dot_general(g, g, NT, preferred_element_type=jnp.float32) * scale)
        packed = jnp.where(rr >= cc, squares[0], squares[1])
        diag = jnp.sum(jnp.where(rr == cc, squares[1], 0.0), axis=0, keepdims=True)
        tail = jnp.broadcast_to(diag, (EXTRA, BF))
        for c in range(CORES):
            for i in range(n_x):
                at = (c * n_x + i) * chunk
                part[k, c, i, 0:chunk, :] = packed[at:at + chunk]
                part[k, c, i, chunk:chunk + EXTRA, :] = tail

    def copy1(k):
        return pltpu.make_async_remote_copy(
            src_ref=part.at[k, 1 - mc], dst_ref=r1.at[k],
            send_sem=s1.at[k], recv_sem=v1.at[k],
            device_id=(me, mx * CORES + 1 - mc), device_id_type=MESH)

    def copy2(k, d):
        to = lax.rem(mx + d, n_x)
        return pltpu.make_async_remote_copy(
            src_ref=held.at[k, to], dst_ref=r2.at[k, d - 1],
            send_sem=s2.at[k, d - 1], recv_sem=v2.at[k, d - 1],
            device_id=(me, to * CORES + mc), device_id_type=MESH)

    def copy3(k):
        return pltpu.make_async_remote_copy(
            src_ref=mine.at[k], dst_ref=r3.at[k],
            send_sem=s3.at[k], recv_sem=v3.at[k],
            device_id=(lax.rem(me + 1 + k, n_aux), oc), device_id_type=MESH)

    def copy4(e):
        return pltpu.make_async_remote_copy(
            src_ref=fin.at[spot], dst_ref=fin.at[spot],
            send_sem=s4.at[e - 1], recv_sem=v4.at[e - 1],
            device_id=(me, lax.rem(oc + e, n_occ)), device_id_type=MESH)

    pairs = n_aux // 2

    def step(t, _):
        @pl.when(t < pairs)
        def _():
            compute(2 * t)
            compute(2 * t + 1)
            copy1(2 * t).start()
            copy1(2 * t + 1).start()

        @pl.when(jnp.logical_and(t >= LAG1, t < pairs + LAG1))
        def _():
            for i in range(2):
                k = 2 * (t - LAG1) + i
                copy1(k).wait_recv()
                held[k] = part[k, mc] + r1[k]
                for d in range(1, n_x):
                    copy2(k, d).start()

        @pl.when(t >= LAG2)
        def _():
            for i in range(2):
                k = 2 * (t - LAG2) + i
                total = held[k, mx]
                for d in range(1, n_x):
                    copy2(k, d).wait_recv()
                    total = total + r2[k, d - 1]
                mine[k] = total

                @pl.when(k < n_aux - 1)
                def _():
                    copy3(k).start()
        return 0

    lax.fori_loop(0, pairs + LAG2, step, 0)

    def gather3(k, total):
        copy3(k).wait_recv()
        return total + r3[k]

    fin[spot] = lax.fori_loop(0, n_aux - 1, gather3, mine[n_aux - 1])
    for e in range(1, n_occ):
        copy4(e).start()

    def drain(k, _):
        copy1(k).wait_send()
        for d in range(1, n_x):
            copy2(k, d).wait_send()

        @pl.when(k < n_aux - 1)
        def _():
            copy3(k).wait_send()
        return 0

    lax.fori_loop(0, n_aux, drain, 0)
    for e in range(n_occ - 1):
        c_copy(e).wait_send()
    for e in range(1, n_occ):
        copy4(e).wait_recv()
    whole = jnp.concatenate([fin[i, 0:chunk, :] for i in range(n_occ)], axis=0)
    turned = whole.T
    out[:, 0, :] = jnp.where(rr >= cc, whole, turned)
    out[:, 1, :] = jnp.where(rr == cc, fin[0, chunk:chunk + 1, :], jnp.where(rr < cc, whole, turned))
    for e in range(1, n_occ):
        copy4(e).wait_send()


def body(integrals, metric_factor, coefficients, owners, row_block, column_block, screen_counts):
    n_aux, n_occ = lax.axis_size("aux"), lax.axis_size("occ")
    slots, aux_local, flat = integrals.shape
    nbasis, occ_local = coefficients.shape
    stacked = integrals.reshape(slots, aux_local, BF, BF).transpose(0, 2, 1, 3).reshape(slots, aux_local * BF, BF)
    n_x = n_occ // CORES
    rows = BF // n_occ + EXTRA
    occ_all = n_occ * occ_local
    dma = pltpu.SemaphoreType.DMA
    f32, bf16 = jnp.float32, jnp.bfloat16
    vmem = pl.BlockSpec(memory_space=pltpu.VMEM)
    hbm = pl.BlockSpec(memory_space=pl.ANY)
    flops = 2 * slots * aux_local * BF * (256 * BF + 2 * BF * occ_all)
    out = pl.pallas_call(
        functools.partial(kernel, n_aux, n_occ),
        out_shape=jax.ShapeDtypeStruct((BF, NBLK_DEV, BF), f32),
        in_specs=[hbm] * 7,
        out_specs=vmem,
        scratch_shapes=[
            pltpu.SMEM(row_block.shape, jnp.int32),
            pltpu.SMEM(row_block.shape, jnp.int32),
            pltpu.SMEM(row_block.shape, jnp.int32),
            pltpu.SMEM(row_block.shape, jnp.int32),
            pltpu.VMEM(metric_factor.shape, bf16),
            dma((5,)),
            pltpu.VMEM((slots, aux_local * BF, BF), bf16),
            pltpu.VMEM((slots, aux_local, BF, BF), bf16),
            pltpu.VMEM((n_occ, nbasis // BF, occ_local, BF), bf16),
            pltpu.VMEM((256, 256), bf16),
            pltpu.VMEM((n_aux, CORES, n_x, rows, BF), f32),
            pltpu.VMEM((n_aux, n_x, rows, BF), f32),
            pltpu.VMEM((n_aux, n_x, rows, BF), f32),
            pltpu.VMEM((n_aux, n_x - 1, rows, BF), f32),
            pltpu.VMEM((n_aux, rows, BF), f32),
            pltpu.VMEM((n_aux - 1, rows, BF), f32),
            pltpu.VMEM((n_occ, rows, BF), f32),
            dma((slots,)), dma((nbasis // BF,)),
            dma((n_occ - 1,)), dma((n_occ - 1,)),
            dma((n_aux,)), dma((n_aux,)),
            dma((n_aux, n_x - 1)), dma((n_aux, n_x - 1)),
            dma((n_aux - 1,)), dma((n_aux - 1,)),
            dma((n_occ - 1,)), dma((n_occ - 1,)),
        ],
        compiler_params=pltpu.CompilerParams(
            collective_id=0, has_side_effects=True, vmem_limit_bytes=61 * 1024 * 1024),
        cost_estimate=pl.CostEstimate(
            flops=flops, bytes_accessed=integrals.size * 2, transcendentals=0),
    )(owners.reshape(-1), row_block, column_block, screen_counts, stacked, metric_factor, coefficients.T)
    return out.transpose(1, 0, 2).reshape(NBLK_DEV, BF * BF)


def solution(mesh):
    return jax.shard_map(
        body,
        mesh=mesh,
        in_specs=(
            P("aux", "occ", None),
            P(("aux", "occ"), None),
            P(None, "occ"),
            P(),
            P(),
            P(),
            P(),
        ),
        out_specs=P("aux", None),
        check_vma=False,
    )
```
